32 devices in a mesh: front: 2 (over core), row: 4 (over y, x), col: 4 (over z).
Axes of the slice: x: 2, y: 2, z: 4, core: 2. Of those that a mesh axis runs over, the one named last changes fastest.
Arguments:
- front_block: float32 [2, 8192, 8192], P('front', 'row', 'col'), as said below
- child_tiles: float32 [2, 224, 16, 128], P('front', ('row', 'col')), may hold values from -3 to 3
- child_rows: int32 [2, 224, 16], P('front', ('row', 'col')), may hold values from 0 to 2047
- child_cols: int32 [2, 224, 128], P('front', ('row', 'col')), may hold values from 0 to 2047
- child_owner: int32 [2, 224], P('front', ('row', 'col')), may hold values from 0 to 15, as said below
Outputs:
- updated_front: float32 [2, 8192, 8192], P('front', 'row', 'col')
The draws below stay inside these ranges and needn't reach their ends.
Inputs may be any that keep to these rules, and one draw needn't show every extreme that they name: `child_owner`: among the tiles of one device no owner appears more than 2 times; in every front some owner gets exactly 2 tiles from every device. `front_block`: the leading 1024 x 1024 block of each assembled front has a symmetric part that is positive definite.
All inputs are finite; a program needn't handle non-finite values.
Results may differ from the reference program's by a relative error of at most 0.0001.
Values sent between devices are 32-bit elements; how exact they have to be, the bound alone decides.
No kernel may reach another device: no remote copies, remote signals or barrier semaphores. Data moves between devices by JAX's collectives and lax.ppermute only.
A program may use at most 256 MiB of HBM per device.

```python
import math
import jax
import jax.numpy as jnp
from jax import lax

F = 8192
P_SIZE = 1024
DB = 128
CR = 16
CC = 128
CAP = 2
NCH = 14
BR = 2048
BC = 2048
N_ROW = 4
N_COL = 4


def draw_front_block(key, part):
    key = jax.random.fold_in(key, 3)
    noise_key, ridge_key = jax.random.split(key)
    noise = jax.random.normal(noise_key, (2, F, F), jnp.float32)
    ridge = jax.random.uniform(ridge_key, (2, F), jnp.float32, 4.0, 5.0) * math.sqrt(P_SIZE)
    places = jnp.arange(F)
    on_diagonal = (places[:, None] == places[None, :]).astype(jnp.float32)
    return noise + ridge[:, :, None] * on_diagonal[None, :, :]


def draw_child_owner(key, part):
    key = jax.random.fold_in(key, 7)
    groups_total = N_ROW * N_COL
    hot_key, rest_key = jax.random.split(key)
    hot_owner = jax.random.randint(hot_key, (2,), 0, groups_total)
    tile_keys = jax.random.split(rest_key, 2 * groups_total)

    def pick_owners(sub_key, hot_dest):
        perm_key, mix_key = jax.random.split(sub_key)
        shuffled = jax.random.permutation(perm_key, groups_total)
        places = jnp.arange(groups_total)
        swapped = jnp.where(shuffled == hot_dest, shuffled[0], shuffled)
        swapped = jnp.where(places == 0, hot_dest, swapped)
        targets = swapped[jnp.arange(NCH) // CAP]
        return targets[jax.random.permutation(mix_key, NCH)]
    hot_all = jnp.repeat(hot_owner, groups_total)
    result = jax.vmap(pick_owners)(tile_keys, hot_all)
    return result.reshape(2, groups_total * NCH).astype(jnp.int32)


def place_ends(values, stream_key, low, high):
    shape = values.shape
    place = [jax.random.randint(jax.random.fold_in(stream_key, axis), (), 0, shape[axis]) for axis in range(len(shape))]
    values = values.at[tuple(place)].set(low)
    longest = shape.index(max(shape))
    place[longest] = (place[longest] + 1) % shape[longest]
    return values.at[tuple(place)].set(high)


def steps_of(own_key, extent, pieces, least, high):
    level = 1.0
    for axis_at, shards_of in pieces:
        steps = jax.random.uniform(jax.random.fold_in(jax.random.fold_in(own_key, 6), axis_at), (shards_of,), jnp.float32, least / len(pieces), high / len(pieces))
        level = level * jnp.repeat(jnp.exp(steps), extent[axis_at] // shards_of).reshape((-1,) + (1,) * (len(extent) - 1 - axis_at))
    return level


def centred(own_key, dims, deviation, bound, shards=(), kind=jnp.bfloat16):
    drawn = jax.random.normal(own_key, dims, jnp.float32) * deviation
    if len(shards) > 0:
        drawn = steps_of(own_key, dims, shards, -0.22, 0.18) * drawn
    return jnp.clip(drawn, min=-bound, max=bound).astype(kind)


def setup_inputs(seed: int = 0) -> dict:
    keys = jax.random.split(jax.random.key(seed), 6)
    front_block = draw_front_block(jax.random.fold_in(keys[5], 71), 0)
    child_tiles = centred(keys[1], (2, N_ROW * N_COL * NCH, CR, CC), 0.5, 3.0, ((0, 2), (1, 16)), jnp.float32)
    child_rows = place_ends(jax.random.randint(keys[2], (2, N_ROW * N_COL * NCH, CR), 0, BR), jax.random.fold_in(keys[2], 1), 0, BR - 1).astype(jnp.int32)
    child_cols = place_ends(jax.random.randint(keys[3], (2, N_ROW * N_COL * NCH, CC), 0, BC), jax.random.fold_in(keys[3], 1), 0, BC - 1).astype(jnp.int32)
    child_owner = draw_child_owner(jax.random.fold_in(keys[5], 71), 0)
    return {"front_block": front_block, "child_tiles": child_tiles, "child_rows": child_rows, "child_cols": child_cols, "child_owner": child_owner}


def blocked_factor(symmetric):
    count = symmetric.shape[0] // DB
    remaining = symmetric
    columns = []
    inverses = []
    identity = jnp.eye(DB, dtype=symmetric.dtype)
    for step in range(count):
        start = step * DB
        chol = jnp.linalg.cholesky(remaining[:DB, :DB])
        inverse = lax.linalg.triangular_solve(chol, identity, left_side=True, lower=True)
        below = jnp.dot(remaining[DB:, :DB], inverse.T, precision=lax.Precision.HIGHEST)
        remaining = remaining[DB:, DB:] - jnp.dot(below, below.T, precision=lax.Precision.HIGHEST)
        columns.append(jnp.concatenate([jnp.zeros((start, DB), symmetric.dtype), chol, below], 0))
        inverses.append(inverse)
    return (jnp.concatenate(columns, 1), inverses)

def blocked_solve(panel, factor, inverses):
    solved_parts = []
    for step in range(len(inverses)):
        start = step * DB
        rhs = panel[:, start:start + DB]
        if step > 0:
            earlier = jnp.concatenate(solved_parts, 1)
            rhs = rhs - jnp.dot(earlier, factor[start:start + DB, :start].T, precision=lax.Precision.HIGHEST)
        solved_parts.append(jnp.dot(rhs, inverses[step].T, precision=lax.Precision.HIGHEST))
    return jnp.concatenate(solved_parts, 1)

def assemble(front_full, piece_tiles, piece_rows, piece_cols, owners):
    global_row = piece_rows + (owners // N_COL * BR)[:, None]
    global_col = piece_cols + (owners % N_COL * BC)[:, None]
    groups_total = N_ROW * N_COL

    def add_block(assembled, members):
        member_tiles, member_rows, member_cols = members
        return (assembled.at[member_rows[:, :, None], member_cols[:, None, :]].add(member_tiles), None)
    assembled, _ = lax.scan(add_block, front_full, (piece_tiles.reshape(groups_total, NCH, CR, CC), global_row.reshape(groups_total, NCH, CR), global_col.reshape(groups_total, NCH, CC)))
    return assembled

def panel_step(assembled):
    diag_block = assembled[:P_SIZE, :P_SIZE]
    symmetric = 0.5 * (diag_block + diag_block.T)
    factor, inverses = blocked_factor(symmetric)
    solved = blocked_solve(assembled[P_SIZE:, :P_SIZE], factor, inverses)
    schur_block = assembled[P_SIZE:, P_SIZE:] - jnp.dot(solved, solved.T, precision=lax.Precision.HIGHEST)
    left_part = jnp.concatenate([factor, solved], 0)
    right_part = jnp.concatenate([assembled[:P_SIZE, P_SIZE:], schur_block], 0)
    return jnp.concatenate([left_part, right_part], 1)

def reference(front_block, child_tiles, child_rows, child_cols, child_owner):
    results = []
    for member in range(2):
        assembled = assemble(front_block[member], child_tiles[member], child_rows[member], child_cols[member], child_owner[member])
        results.append(panel_step(assembled))
    return jnp.stack(results, 0)
```

```python
import functools
import jax
import jax.numpy as jnp
from jax import lax
from jax.experimental import pallas as pl
from jax.experimental.pallas import tpu as pltpu
from jax.sharding import PartitionSpec as P

P_SIZE = 1024
DB = 128
CR = 16
CC = 128
CAP = 2
GROUP = 8
WIDE = 512
SLOT = 24
CHUNKS = 8
STRIP = 256
MIB = 2**20
GRID = ("row", "col")
HIGHEST = lax.Precision.HIGHEST
VMEM = pltpu.VMEM
F32 = jnp.float32
BF16 = jnp.bfloat16


def spread(array, axis, root):
    mine = lax.axis_index(axis) == root
    return lax.psum(jnp.where(mine, array, jnp.zeros_like(array)), axis)


def of_lane(tile, at):
    return jnp.broadcast_to(tile[:, at : at + 1], tile.shape)


def of_row(tile, at):
    return jnp.broadcast_to(tile[at : at + 1, :], tile.shape)


def reciprocal(value):
    guess = pl.reciprocal(value, approx=True)
    guess = guess * (2.0 - value * guess)
    return guess * (2.0 - value * guess)


def tree_sum(terms):
    while len(terms) > 1:
        terms = [terms[at] + terms[at + 1] for at in range(0, len(terms), 2)]
    return terms[0]


def factor_tile(w):
    n = DB // GROUP
    row = lax.broadcasted_iota(jnp.int32, (GROUP, DB), 0)
    col = lax.broadcasted_iota(jnp.int32, (GROUP, DB), 1)
    x = [jnp.where(col == row + GROUP * i, 1.0, 0.0).astype(F32) for i in range(n)]
    upper, inverse = [], []
    for g in range(n):
        first = GROUP * g
        lanes = [of_lane(w[g], first + m) for m in range(GROUP)]
        s = {(k, m): of_row(lanes[m], k) for m in range(GROUP) for k in range(m + 1)}
        rw = [of_row(w[g], k) for k in range(GROUP)]
        rx = [of_row(x[g], k) for k in range(GROUP)]
        l, rec = {}, []
        for k in range(GROUP):
            rec.append(reciprocal(s[k, k]))
            for i in range(k + 1, GROUP):
                l[i, k] = s[k, i] * rec[k]
            for i in range(k + 1, GROUP):
                for m in range(i, GROUP):
                    s[i, m] = s[i, m] - l[i, k] * s[k, m]
                rw[i] = rw[i] - l[i, k] * rw[k]
                rx[i] = rx[i] - l[i, k] * rx[k]
        scale = [lax.rsqrt(s[k, k]) for k in range(GROUP)]
        up, inv = rw[0] * scale[0], rx[0] * scale[0]
        for k in range(1, GROUP):
            up = jnp.where(row == k, rw[k] * scale[k], up)
            inv = jnp.where(row == k, rx[k] * scale[k], inv)
        upper.append(jnp.where(col >= row + first, up, 0.0))
        inverse.append(inv)
        if g + 1 == n:
            break
        qw = [rw[k] * rec[k] for k in range(GROUP)]
        qx = [rx[k] * rec[k] for k in range(GROUP)]
        for k in reversed(range(GROUP)):
            for i in range(k):
                qw[i] = qw[i] - l[k, i] * qw[k]
                qx[i] = qx[i] - l[k, i] * qx[k]
        for i in range(g + 1, n):
            at = [of_lane(w[i], first + m) for m in range(GROUP)]
            w[i] = w[i] - tree_sum([at[m] * qw[m] for m in range(GROUP)])
            x[i] = x[i] - tree_sum([at[m] * qx[m] for m in range(GROUP)])
    return upper, inverse


def dot(a, b, dims=((1,), (0,))):
    return lax.dot_general(a, b, (dims, ((), ())), precision=HIGHEST, preferred_element_type=F32)


NT = ((1,), (1,))
TN = ((0,), (0,))


def factor_kernel(blocks, a_ref, l_ref, z_ref, u_ref, d_ref):
    def block(i):
        return pl.ds(pl.multiple_of(i * DB, DB), DB)

    def symmetric(i, _):
        def one(j, _):
            z_ref[block(i), block(j)] = 0.5 * (a_ref[block(i), block(j)] + a_ref[block(j), block(i)].T)
            return 0

        lax.fori_loop(0, blocks, one, 0)
        return 0

    lax.fori_loop(0, blocks, symmetric, 0)

    def step(j, _):
        now = block(j)
        base = pl.multiple_of(j * DB, DB)
        tiles = [
            z_ref[pl.ds(pl.multiple_of(base + GROUP * i, GROUP), GROUP), now]
            for i in range(DB // GROUP)
        ]
        upper, inverse = factor_tile(tiles)
        for i in range(DB // GROUP):
            u_ref[GROUP * i : GROUP * i + GROUP, now] = upper[i]
            d_ref[GROUP * i : GROUP * i + GROUP, :] = inverse[i]
            z_ref[pl.ds(pl.multiple_of(base + GROUP * i, GROUP), GROUP), now] = inverse[i]
        m = d_ref[...]
        l_ref[now, now] = u_ref[:, now].T
        for c in range(0, blocks * DB, WIDE):
            u_ref[:, c : c + WIDE] = dot(m, z_ref[now, c : c + WIDE])
        u_ref[:, now] = m
        z_ref[now, :] = u_ref[...]

        def trail(i, _):
            below = block(i)
            ui = u_ref[:, below]
            l_ref[below, now] = ui.T
            l_ref[now, below] = jnp.zeros((DB, DB), F32)
            z_ref[below, now] = jnp.zeros((DB, DB), F32)
            for c in range(0, blocks * DB, WIDE):
                z_ref[below, c : c + WIDE] = z_ref[below, c : c + WIDE] - dot(
                    ui, u_ref[:, c : c + WIDE], TN
                )
            return 0

        lax.fori_loop(j + 1, blocks, trail, 0)
        return 0

    lax.fori_loop(0, blocks, step, 0)

    def clean(i, _):
        def one(j, _):
            z_ref[block(i), block(j)] = jnp.zeros((DB, DB), F32)
            return 0

        lax.fori_loop(i + 1, blocks, one, 0)
        return 0

    lax.fori_loop(0, blocks, clean, 0)


def maybe_factor_kernel(blocks, holds_ref, a_ref, *rest):
    @pl.when(holds_ref[0] == 1)
    def _():
        factor_kernel(blocks, a_ref, *rest)


def factor(block, holds):
    size = block.shape[0]
    return pl.pallas_call(
        functools.partial(maybe_factor_kernel, size // DB),
        out_shape=[jax.ShapeDtypeStruct((size, size), F32)] * 2,
        in_specs=[pl.BlockSpec(memory_space=pltpu.SMEM), pl.BlockSpec(memory_space=VMEM)],
        out_specs=[pl.BlockSpec(memory_space=VMEM)] * 2,
        scratch_shapes=[VMEM((DB, size), F32), VMEM((DB, DB), F32)],
        compiler_params=pltpu.CompilerParams(vmem_limit_bytes=40 * MIB),
        name="panel_factor",
    )(jnp.full((1,), holds, jnp.int32), block)


def pack_kernel(groups, owner_ref, tile_ref, row_ref, col_ref, out_ref, seen_ref):
    out_ref[...] = jnp.zeros_like(out_ref)
    for group in range(groups):
        seen_ref[group] = 0

    def place(t, _):
        owner = owner_ref[t]
        rank = seen_ref[owner]
        seen_ref[owner] = rank + 1
        slot = owner * CAP + rank
        out_ref[slot, 0:CR, :] = tile_ref[t]
        out_ref[slot, CR : CR + 1, :] = col_ref[t].astype(F32)
        out_ref[slot, CR + 1 : CR + 2, :] = row_ref[t].astype(F32)
        return 0

    lax.fori_loop(0, tile_ref.shape[0], place, 0)


def pack(tiles, rows, cols, owners, groups):
    count = owners.shape[0]
    rows = jnp.pad(rows, ((0, 0), (0, CC - CR))).reshape(count, 1, CC)
    return pl.pallas_call(
        functools.partial(pack_kernel, groups),
        out_shape=jax.ShapeDtypeStruct((groups * CAP, SLOT, CC), F32),
        in_specs=[pl.BlockSpec(memory_space=pltpu.SMEM)] + [pl.BlockSpec(memory_space=VMEM)] * 3,
        out_specs=pl.BlockSpec(memory_space=VMEM),
        scratch_shapes=[pltpu.SMEM((groups,), jnp.int32)],
        name="pack_tiles",
    )(owners, tiles, rows, cols.reshape(count, 1, CC))


def halves(value):
    high = value.astype(BF16)
    return high, (value - high.astype(F32)).astype(BF16)


def mm(a, b, dims):
    return lax.dot_general(a, b, (dims, ((), ())), preferred_element_type=F32)


def expand_kernel(slots_ref, high_ref, low_ref):
    cols = high_ref.shape[0]
    place = lax.broadcasted_iota(jnp.int32, (cols, 2 * CC), 0)
    row = lax.broadcasted_iota(jnp.int32, (CC, CC), 0) // CR
    total = jnp.zeros((cols, 2 * CC), F32)
    for pair in range(0, 8, 2):
        index = jnp.concatenate([slots_ref[pair + k, CR : CR + 1, :] for k in range(2)], 1)
        onehot = jnp.where(place == index.astype(jnp.int32), 1.0, 0.0).astype(BF16)
        highs, lows = [], []
        for k in range(2):
            tile = slots_ref[pair + k, 0:CR, :]
            tall = jnp.concatenate([tile] * (CC // CR), 0)
            high, low = halves(jnp.where(row == pair + k, tall, 0.0))
            highs.append(high)
            lows.append(low)
        packed = jnp.concatenate([jnp.concatenate(highs, 1), jnp.concatenate(lows, 1)], 0)
        total = total + mm(onehot, packed, NT)
    high, low = halves(total[:, :CC] + total[:, CC:])
    high_ref[...] = high
    low_ref[...] = low


def expand(slots, cols):
    count = slots.shape[0]
    return pl.pallas_call(
        expand_kernel,
        grid=(count // 8,),
        out_shape=[jax.ShapeDtypeStruct((cols, count * CR), BF16)] * 2,
        in_specs=[pl.BlockSpec((8, SLOT, CC), lambda g: (g, 0, 0))],
        out_specs=[pl.BlockSpec((cols, CC), lambda g: (0, g))] * 2,
        compiler_params=pltpu.CompilerParams(vmem_limit_bytes=40 * MIB),
        name="expand_columns",
    )(slots)


def assemble_kernel(step, rows_ref, high_ref, low_ref, front_ref, out_ref):
    first = pl.program_id(0) * step
    place = lax.broadcasted_iota(jnp.int32, (step, rows_ref.shape[1]), 0) + first
    onehot = jnp.where(place == rows_ref[...], 1.0, 0.0).astype(BF16)
    out_ref[...] = front_ref[...] + (mm(onehot, high_ref[...], NT) + mm(onehot, low_ref[...], NT))


def assemble(front, rows, high, low):
    step = 256
    count, width = front.shape
    k = rows.shape[1]
    return pl.pallas_call(
        functools.partial(assemble_kernel, step),
        grid=(count // step,),
        out_shape=jax.ShapeDtypeStruct((count, width), F32),
        in_specs=[
            pl.BlockSpec((1, k), lambda i: (0, 0)),
            pl.BlockSpec((width, k), lambda i: (0, 0)),
            pl.BlockSpec((width, k), lambda i: (0, 0)),
            pl.BlockSpec((step, width), lambda i: (i, 0)),
        ],
        out_specs=pl.BlockSpec((step, width), lambda i: (i, 0)),
        compiler_params=pltpu.CompilerParams(vmem_limit_bytes=40 * MIB),
        name="assemble",
    )(rows, high, low, front)


def solve_kernel(rows_ref, *refs):
    strips = refs[: P_SIZE // STRIP]
    out_high_ref, out_low_ref, high_ref, low_ref = refs[P_SIZE // STRIP :]

    @pl.when(pl.program_id(0) == 0)
    def _():
        for i, strip in enumerate(strips):
            c, upto = i * STRIP, (i + 1) * STRIP
            high_ref[c:upto, :upto], low_ref[c:upto, :upto] = halves(strip[...])

    for c in range(0, P_SIZE, STRIP):
        upto = c + STRIP
        a, b = halves(rows_ref[:, :upto])
        high, low = high_ref[c:upto, :upto], low_ref[c:upto, :upto]
        part = mm(a, high, NT) + (mm(a, low, NT) + mm(b, high, NT))
        out_high_ref[:, c:upto], out_low_ref[:, c:upto] = halves(part)


def solve(rows, strips):
    step = min(512, rows.shape[0])
    part = pl.BlockSpec((step, P_SIZE), lambda i: (i, 0))
    return pl.pallas_call(
        solve_kernel,
        grid=(rows.shape[0] // step,),
        out_shape=[jax.ShapeDtypeStruct(rows.shape, BF16)] * 2,
        in_specs=[part] + [pl.BlockSpec(strip.shape, lambda i: (0, 0)) for strip in strips],
        out_specs=[part, part],
        scratch_shapes=[VMEM((P_SIZE, P_SIZE), BF16)] * 2,
        compiler_params=pltpu.CompilerParams(vmem_limit_bytes=40 * MIB),
        name="solve_rows",
    )(rows, *strips)


def update_kernel(step, place_ref, rh_ref, rl_ref, ch_ref, cl_ref, front_ref, factor_ref, out_ref):
    above = (place_ref[0] == 0) & (pl.program_id(0) * step < P_SIZE)
    first_col = place_ref[1] == 0
    width = out_ref.shape[1]

    def schur(left):
        a, b = rh_ref[...], rl_ref[...]
        for c in range(left, width, WIDE):
            high, low = ch_ref[c : c + WIDE, :], cl_ref[c : c + WIDE, :]
            part = mm(a, high, NT) + (mm(a, low, NT) + mm(b, high, NT))
            out_ref[:, c : c + WIDE] = front_ref[:, c : c + WIDE] - part

    @pl.when(above)
    def _():
        out_ref[...] = front_ref[...]

        @pl.when(first_col)
        def _():
            out_ref[:, :P_SIZE] = factor_ref[...]

    @pl.when(jnp.logical_not(above) & first_col)
    def _():
        out_ref[:, :P_SIZE] = rh_ref[...].astype(F32) + rl_ref[...].astype(F32)
        schur(P_SIZE)

    @pl.when(jnp.logical_not(above) & jnp.logical_not(first_col))
    def _():
        schur(0)


def update(place, row_parts, col_parts, front, factor_rows):
    step = 256
    count, width = front.shape
    row = pl.BlockSpec((step, P_SIZE), lambda i: (i, 0))
    whole = pl.BlockSpec((width, P_SIZE), lambda i: (0, 0))
    wide = pl.BlockSpec((step, width), lambda i: (i, 0))
    last = P_SIZE // step - 1
    return pl.pallas_call(
        functools.partial(update_kernel, step),
        grid=(count // step,),
        out_shape=jax.ShapeDtypeStruct((count, width), F32),
        in_specs=[
            pl.BlockSpec(memory_space=pltpu.SMEM),
            row,
            row,
            whole,
            whole,
            wide,
            pl.BlockSpec((step, P_SIZE), lambda i: (jnp.minimum(i, last), 0)),
        ],
        out_specs=wide,
        compiler_params=pltpu.CompilerParams(vmem_limit_bytes=56 * MIB),
        name="schur_update",
    )(place, *row_parts, *col_parts, front, factor_rows)


def pairs_of(route, rows, cols, col_count):
    return [
        (r * col_count + c, to[0] * col_count + to[1])
        for r in rows
        for c in cols
        for to in [route(r, c)]
        if to is not None
    ]


def down_columns(part, col, rows):
    moves = [[(r * 4 + a, r * 4 + b) for r in rows] for a, b in ((0, 2), (2, 1), (2, 3))]
    middle = lax.ppermute(part, GRID, moves[0])
    one = lax.ppermute(middle, GRID, moves[1])
    three = lax.ppermute(middle, GRID, moves[2])
    return jnp.where(col == 0, part, jnp.where(col == 2, middle, jnp.where(col == 1, one, three)))


def in_plane(part, row, col, cols, source, hops):
    held = part
    result = part
    at = 0
    for hop in hops:
        pairs = [((source(c) ^ at) * 4 + c, (source(c) ^ at ^ hop) * 4 + c) for c in cols]
        held = lax.ppermute(held, GRID, pairs)
        at ^= hop
        result = jnp.where(row == (source(col) ^ at), held, result)
    return result


def fast_local(front_block, child_tiles, child_rows, child_cols, child_owner):
    front = front_block[0]
    block_rows, block_cols = front.shape
    row = lax.axis_index("row")
    col = lax.axis_index("col")
    slots = pack(child_tiles[0], child_rows[0], child_cols[0], child_owner[0], 16)
    slots = lax.all_to_all(slots, GRID, split_axis=0, concat_axis=0, tiled=True)
    rows = slots[:, CR + 1, :CR].astype(jnp.int32).reshape(1, -1)
    high, low = expand(slots, block_cols)
    assembled = assemble(front, rows, high, low)
    holds = ((row == 0) & (col == 0)).astype(jnp.int32)
    factor_rows, inverse = factor(assembled[:P_SIZE, :P_SIZE], holds)
    strips = []
    for c in range(0, P_SIZE, STRIP):
        strip = inverse[c : c + STRIP, : c + STRIP]
        strip = down_columns(strip, col, (0,))
        one = lax.ppermute(strip, GRID, [(c, 4 + c) for c in range(4)])
        two = lax.ppermute(strip, GRID, [(c, 8 + c) for c in range(4)])
        three = lax.ppermute(one, GRID, [(4 + c, 12 + c) for c in range(4)])
        strip = jnp.where(row == 0, strip, jnp.where(row == 1, one, jnp.where(row == 2, two, three)))
        strips.append(strip)
    size = block_rows // CHUNKS
    row_chunks, col_chunks = [], []
    for at in range(CHUNKS):
        top = at * size
        part = assembled[top : top + size, :P_SIZE]
        top_rows = top < P_SIZE
        part = down_columns(part, col, (1, 2, 3) if top_rows else (0, 1, 2, 3))
        row_chunks.append(part)
        half = size // 2
        cols = (1, 2, 3) if top_rows else (0, 1, 2, 3)
        source = lambda c: c
        first = in_plane(part[:half], row, col, cols, source, (1, 2, 1))
        second = in_plane(part[half:], row, col, cols, source, (2, 1, 2))
        col_chunks += [first, second]
    row_solved = solve(jnp.concatenate(row_chunks, 0), strips)
    col_solved = solve(jnp.concatenate(col_chunks, 0), strips)
    place = jnp.stack([row, col]).astype(jnp.int32)
    return update(place, row_solved, col_solved, assembled, factor_rows)[None]


def blocked_factor(symmetric):
    count = symmetric.shape[0] // DB
    remaining = symmetric
    columns = []
    inverses = []
    identity = jnp.eye(DB, dtype=symmetric.dtype)
    for step in range(count):
        start = step * DB
        chol = jnp.linalg.cholesky(remaining[:DB, :DB])
        inverse = lax.linalg.triangular_solve(chol, identity, left_side=True, lower=True)
        below = jnp.dot(remaining[DB:, :DB], inverse.T, precision=lax.Precision.HIGHEST)
        remaining = remaining[DB:, DB:] - jnp.dot(below, below.T, precision=lax.Precision.HIGHEST)
        columns.append(jnp.concatenate([jnp.zeros((start, DB), symmetric.dtype), chol, below], 0))
        inverses.append(inverse)
    return (jnp.concatenate(columns, 1), inverses)


def blocked_solve(panel, factor, inverses):
    solved_parts = []
    for step in range(len(inverses)):
        start = step * DB
        rhs = panel[:, start : start + DB]
        if step > 0:
            earlier = jnp.concatenate(solved_parts, 1)
            rhs = rhs - jnp.dot(
                earlier, factor[start : start + DB, :start].T, precision=lax.Precision.HIGHEST
            )
        solved_parts.append(jnp.dot(rhs, inverses[step].T, precision=lax.Precision.HIGHEST))
    return jnp.concatenate(solved_parts, 1)


def local(front_block, child_tiles, child_rows, child_cols, child_owner):
    front_part = front_block[0]
    child_part = child_tiles[0]
    row_maps = child_rows[0]
    col_maps = child_cols[0]
    owners = child_owner[0]
    row_count = lax.axis_size("row")
    col_count = lax.axis_size("col")
    group_count = row_count * col_count
    block_rows, block_cols = front_part.shape
    tile_count = owners.shape[0]
    positions = jnp.arange(tile_count)
    earlier = (owners[:, None] == owners[None, :]) & (positions[None, :] < positions[:, None])
    tile_rank = jnp.sum(earlier.astype(jnp.int32), axis=1)
    slot_index = owners * CAP + tile_rank
    send_tiles = (
        jnp.zeros((group_count * CAP, CR, CC), front_part.dtype).at[slot_index].set(child_part)
    )
    send_rows = jnp.zeros((group_count * CAP, CR), jnp.int32).at[slot_index].set(row_maps)
    send_cols = jnp.zeros((group_count * CAP, CC), jnp.int32).at[slot_index].set(col_maps)
    recv_tiles, recv_rows, recv_cols = (
        lax.all_to_all(send_tiles, ("row", "col"), split_axis=0, concat_axis=0, tiled=True),
        lax.all_to_all(send_rows, ("row", "col"), split_axis=0, concat_axis=0, tiled=True),
        lax.all_to_all(send_cols, ("row", "col"), split_axis=0, concat_axis=0, tiled=True),
    )
    assembled = front_part.at[recv_rows[:, :, None], recv_cols[:, None, :]].add(recv_tiles)
    panel_block = spread(assembled[:, :P_SIZE], "col", 0)
    row_index = lax.axis_index("row")
    col_index = lax.axis_index("col")
    first_row = row_index * block_rows
    held_rows = min(P_SIZE, block_rows)
    holders = max(1, P_SIZE // block_rows)
    diag_pieces = [spread(panel_block[:held_rows], "row", member) for member in range(holders)]
    diag_block = jnp.concatenate(diag_pieces, 0)
    symmetric = 0.5 * (diag_block + diag_block.T)
    factor, inverses = blocked_factor(symmetric)
    solved = blocked_solve(panel_block, factor, inverses)
    global_rows = first_row + jnp.arange(block_rows)
    below_mask = global_rows[:, None] >= P_SIZE
    if block_rows <= P_SIZE:
        factor_rows = lax.dynamic_slice_in_dim(
            factor, jnp.minimum(first_row, P_SIZE - block_rows), block_rows, 0
        )
    else:
        factor_rows = jnp.concatenate(
            [factor, jnp.zeros((block_rows - P_SIZE, P_SIZE), factor.dtype)], 0
        )
    panel_out = jnp.where(below_mask, solved, factor_rows)
    lower_part = jnp.where(below_mask, solved, 0.0)
    group_ratio = row_count // col_count
    column_parts = [
        spread(lower_part, "row", col_index * group_ratio + member) for member in range(group_ratio)
    ]
    column_part = jnp.concatenate(column_parts, 0)
    schur_block = assembled - jnp.dot(lower_part, column_part.T, precision=lax.Precision.HIGHEST)
    global_cols = col_index * block_cols + jnp.arange(block_cols)
    left_part = jnp.concatenate(
        [panel_out, jnp.zeros((block_rows, block_cols - P_SIZE), panel_out.dtype)], 1
    )
    trailing = below_mask & (global_cols[None, :] >= P_SIZE)
    updated = jnp.where(
        global_cols[None, :] < P_SIZE, left_part, jnp.where(trailing, schur_block, assembled)
    )
    return updated[None]


def solution(mesh):
    placed = (
        P("front", "row", "col"),
        P("front", ("row", "col"), None, None),
        P("front", ("row", "col"), None),
        P("front", ("row", "col"), None),
        P("front", ("row", "col")),
    )
    square = mesh.shape["row"] == 4 and mesh.shape["col"] == 4
    return jax.shard_map(
        fast_local if square else local,
        mesh=mesh,
        in_specs=placed,
        out_specs=P("front", "row", "col"),
        check_vma=False,
    )
```

```python
import functools
import jax
import jax.numpy as jnp
from jax import lax
from jax.experimental import pallas as pl
from jax.experimental.pallas import tpu as pltpu
from jax.sharding import PartitionSpec as P

P_SIZE = 1024
DB = 128
CR = 16
CC = 128
CAP = 2
GROUP = 8
WIDE = 512
SLOT = 24
CHUNKS = 8
STRIP = 256
MIB = 2**20
GRID = ("row", "col")
HIGHEST = lax.Precision.HIGHEST
VMEM = pltpu.VMEM
F32 = jnp.float32
BF16 = jnp.bfloat16


def spread(array, axis, root):
    mine = lax.axis_index(axis) == root
    return lax.psum(jnp.where(mine, array, jnp.zeros_like(array)), axis)


def of_lane(tile, at):
    return jnp.broadcast_to(tile[:, at : at + 1], tile.shape)


def of_row(tile, at):
    return jnp.broadcast_to(tile[at : at + 1, :], tile.shape)


def reciprocal(value):
    guess = pl.reciprocal(value, approx=True)
    guess = guess * (2.0 - value * guess)
    return guess * (2.0 - value * guess)


def tree_sum(terms):
    while len(terms) > 1:
        terms = [terms[at] + terms[at + 1] for at in range(0, len(terms), 2)]
    return terms[0]


def factor_tile(w):
    n = DB // GROUP
    row = lax.broadcasted_iota(jnp.int32, (GROUP, DB), 0)
    col = lax.broadcasted_iota(jnp.int32, (GROUP, DB), 1)
    x = [jnp.where(col == row + GROUP * i, 1.0, 0.0).astype(F32) for i in range(n)]
    upper, inverse = [], []
    for g in range(n):
        first = GROUP * g
        lanes = [of_lane(w[g], first + m) for m in range(GROUP)]
        s = {(k, m): of_row(lanes[m], k) for m in range(GROUP) for k in range(m + 1)}
        rw = [of_row(w[g], k) for k in range(GROUP)]
        rx = [of_row(x[g], k) for k in range(GROUP)]
        l, rec = {}, []
        for k in range(GROUP):
            rec.append(reciprocal(s[k, k]))
            for i in range(k + 1, GROUP):
                l[i, k] = s[k, i] * rec[k]
            for i in range(k + 1, GROUP):
                for m in range(i, GROUP):
                    s[i, m] = s[i, m] - l[i, k] * s[k, m]
                rw[i] = rw[i] - l[i, k] * rw[k]
                rx[i] = rx[i] - l[i, k] * rx[k]
        scale = [lax.rsqrt(s[k, k]) for k in range(GROUP)]
        up, inv = rw[0] * scale[0], rx[0] * scale[0]
        for k in range(1, GROUP):
            up = jnp.where(row == k, rw[k] * scale[k], up)
            inv = jnp.where(row == k, rx[k] * scale[k], inv)
        upper.append(jnp.where(col >= row + first, up, 0.0))
        inverse.append(inv)
        if g + 1 == n:
            break
        qw = [rw[k] * rec[k] for k in range(GROUP)]
        qx = [rx[k] * rec[k] for k in range(GROUP)]
        for k in reversed(range(GROUP)):
            for i in range(k):
                qw[i] = qw[i] - l[k, i] * qw[k]
                qx[i] = qx[i] - l[k, i] * qx[k]
        for i in range(g + 1, n):
            at = [of_lane(w[i], first + m) for m in range(GROUP)]
            w[i] = w[i] - tree_sum([at[m] * qw[m] for m in range(GROUP)])
            x[i] = x[i] - tree_sum([at[m] * qx[m] for m in range(GROUP)])
    return upper, inverse


def dot(a, b, dims=((1,), (0,))):
    return lax.dot_general(a, b, (dims, ((), ())), precision=HIGHEST, preferred_element_type=F32)


NT = ((1,), (1,))
TN = ((0,), (0,))


def factor_step(blocks, j, z_ref, l_ref, u_ref, d_ref, left):
    def block(i):
        return pl.ds(pl.multiple_of(i * DB, DB), DB)

    now = block(j)
    base = pl.multiple_of(j * DB, DB)
    tiles = [
        z_ref[pl.ds(pl.multiple_of(base + GROUP * i, GROUP), GROUP), now] for i in range(DB // GROUP)
    ]
    upper, inverse = factor_tile(tiles)
    for i in range(DB // GROUP):
        u_ref[GROUP * i : GROUP * i + GROUP, now] = upper[i]
        d_ref[GROUP * i : GROUP * i + GROUP, :] = inverse[i]
        z_ref[pl.ds(pl.multiple_of(base + GROUP * i, GROUP), GROUP), now] = inverse[i]
    m = d_ref[...]
    l_ref[now, left] = u_ref[:, now].T
    for c in range(0, blocks * DB, WIDE):
        u_ref[:, c : c + WIDE] = dot(m, z_ref[now, c : c + WIDE])
    u_ref[:, now] = m
    z_ref[now, :] = u_ref[...]

    def trail(i, _):
        below = block(i)
        ui = u_ref[:, below]
        l_ref[below, left] = ui.T
        z_ref[below, now] = jnp.zeros((DB, DB), F32)
        for c in range(0, blocks * DB, WIDE):
            z_ref[below, c : c + WIDE] = z_ref[below, c : c + WIDE] - dot(
                ui, u_ref[:, c : c + WIDE], TN
            )
        return 0

    lax.fori_loop(j + 1, blocks, trail, 0)


def copy(source, target, sem):
    return pltpu.make_async_copy(source, target, sem)


def first_block(front_ref, rows_ref, high_ref, low_ref, a_ref, z_ref, sem):
    size = a_ref.shape[0]
    load = copy(front_ref.at[pl.ds(0, size), pl.ds(0, size)], a_ref, sem)
    load.start()
    load.wait()

    def add(i, _):
        part = pl.ds(pl.multiple_of(i * STRIP, STRIP), STRIP)
        place = lax.broadcasted_iota(jnp.int32, (STRIP, rows_ref.shape[1]), 0) + i * STRIP
        onehot = jnp.where(place == rows_ref[...], 1.0, 0.0).astype(BF16)
        a_ref[part, :] += mm(onehot, high_ref[...], NT) + mm(onehot, low_ref[...], NT)
        return 0

    lax.fori_loop(0, size // STRIP, add, 0)

    def symmetric(i, _):
        def one(j, _):
            bi = pl.ds(pl.multiple_of(i * DB, DB), DB)
            bj = pl.ds(pl.multiple_of(j * DB, DB), DB)
            z_ref[bi, bj] = 0.5 * (a_ref[bi, bj] + a_ref[bj, bi].T)
            return 0

        lax.fori_loop(0, size // DB, one, 0)
        return 0

    lax.fori_loop(0, size // DB, symmetric, 0)


def factor_kernel(top, tall, holds_ref, token_ref, *refs):
    if top == 0:
        front_ref, rows_ref, high_ref, low_ref = refs[:4]
        z_out, l_out, strip_ref, a_ref, z_ref, l_ref, u_ref, d_ref, sem = refs[4:]
    else:
        z_in, l_in, z_out, l_out, strip_ref, z_ref, l_ref, u_ref, d_ref, sem = refs
    size = z_ref.shape[0]
    below = pl.ds(top, size - top)

    def moved(source, target):
        one = copy(source, target, sem)
        one.start()
        one.wait()

    @pl.when(holds_ref[0] == 1)
    def _():
        if top == 0:
            first_block(front_ref, rows_ref, high_ref, low_ref, a_ref, z_ref, sem)
        else:
            moved(z_in.at[below, :], z_ref.at[below, :])
            l_ref[0:top, :] = jnp.zeros((top, tall), F32)
        for k in range(DB, tall, DB):
            l_ref[top + k - DB : top + k, k:] = jnp.zeros((DB, tall - k), F32)
        for k in range(0, tall, DB):
            factor_step(size // DB, (top + k) // DB, z_ref, l_ref, u_ref, d_ref, slice(k, k + DB))
        for k in range(DB, tall, DB):
            z_ref[top + k - DB : top + k, top + k : top + tall] = jnp.zeros((DB, tall - k), F32)
        moved(z_ref.at[pl.ds(top, tall), pl.ds(0, top + tall)], strip_ref)
        moved(l_ref, l_out.at[:, pl.ds(top, tall)])
        if top + tall < size:
            rest = pl.ds(top + tall, size - top - tall)
            moved(z_ref.at[rest, :], z_out.at[rest, :])


def factor(top, tall, holds, token, state, size):
    anywhere = pl.BlockSpec(memory_space=pl.ANY)
    resident = pl.BlockSpec(memory_space=VMEM)
    square = jax.ShapeDtypeStruct((size, size), F32)
    specs = [anywhere] + [resident] * 3 if top == 0 else [anywhere] * 2
    scratch = [VMEM((size, size), F32)] if top == 0 else []
    scratch += [VMEM((size, size), F32), VMEM((size, tall), F32), VMEM((DB, size), F32)]
    scratch += [VMEM((DB, DB), F32), pltpu.SemaphoreType.DMA]
    return pl.pallas_call(
        functools.partial(factor_kernel, top, tall),
        out_shape=[square, square, jax.ShapeDtypeStruct((tall, top + tall), F32)],
        in_specs=[pl.BlockSpec(memory_space=pltpu.SMEM), anywhere] + specs,
        out_specs=[anywhere] * 3,
        scratch_shapes=scratch,
        input_output_aliases={} if top == 0 else {2: 0, 3: 1},
        compiler_params=pltpu.CompilerParams(vmem_limit_bytes=58 * MIB),
        cost_estimate=pl.CostEstimate(flops=10**10, bytes_accessed=2 * 10**7, transcendentals=0),
        name="panel_factor",
    )(holds, token, *state)


def pack_kernel(groups, owner_ref, tile_ref, row_ref, col_ref, out_ref, seen_ref):
    out_ref[...] = jnp.zeros_like(out_ref)
    for group in range(groups):
        seen_ref[group] = 0

    def place(t, _):
        owner = owner_ref[t]
        rank = seen_ref[owner]
        seen_ref[owner] = rank + 1
        slot = owner * CAP + rank
        out_ref[slot, 0:CR, :] = tile_ref[t]
        out_ref[slot, CR : CR + 1, :] = col_ref[t].astype(F32)
        out_ref[slot, CR + 1 : CR + 2, :] = row_ref[t].astype(F32)
        return 0

    lax.fori_loop(0, tile_ref.shape[0], place, 0)


def pack(tiles, rows, cols, owners, groups):
    count = owners.shape[0]
    rows = jnp.pad(rows, ((0, 0), (0, CC - CR))).reshape(count, 1, CC)
    return pl.pallas_call(
        functools.partial(pack_kernel, groups),
        out_shape=jax.ShapeDtypeStruct((groups * CAP, SLOT, CC), F32),
        in_specs=[pl.BlockSpec(memory_space=pltpu.SMEM)] + [pl.BlockSpec(memory_space=VMEM)] * 3,
        out_specs=pl.BlockSpec(memory_space=VMEM),
        scratch_shapes=[pltpu.SMEM((groups,), jnp.int32)],
        name="pack_tiles",
    )(owners, tiles, rows, cols.reshape(count, 1, CC))


def halves(value):
    high = value.astype(BF16)
    return high, (value - high.astype(F32)).astype(BF16)


def mm(a, b, dims):
    return lax.dot_general(a, b, (dims, ((), ())), preferred_element_type=F32)


def expand_kernel(token_ref, slots_ref, high_ref, low_ref):
    cols = high_ref.shape[0]
    place = lax.broadcasted_iota(jnp.int32, (cols, 2 * CC), 0)
    row = lax.broadcasted_iota(jnp.int32, (CC, CC), 0) // CR
    total = jnp.zeros((cols, 2 * CC), F32)
    for pair in range(0, 8, 2):
        index = jnp.concatenate([slots_ref[pair + k, CR : CR + 1, :] for k in range(2)], 1)
        onehot = jnp.where(place == index.astype(jnp.int32), 1.0, 0.0).astype(BF16)
        highs, lows = [], []
        for k in range(2):
            tile = slots_ref[pair + k, 0:CR, :]
            tall = jnp.concatenate([tile] * (CC // CR), 0)
            high, low = halves(jnp.where(row == pair + k, tall, 0.0))
            highs.append(high)
            lows.append(low)
        packed = jnp.concatenate([jnp.concatenate(highs, 1), jnp.concatenate(lows, 1)], 0)
        total = total + mm(onehot, packed, NT)
    high, low = halves(total[:, :CC] + total[:, CC:])
    high_ref[...] = high
    low_ref[...] = low


def expand(slots, cols, token):
    count = slots.shape[0]
    return pl.pallas_call(
        expand_kernel,
        grid=(count // 8,),
        out_shape=[jax.ShapeDtypeStruct((cols, count * CR), BF16)] * 2,
        in_specs=[pl.BlockSpec(memory_space=pl.ANY), pl.BlockSpec((8, SLOT, CC), lambda g: (g, 0, 0))],
        out_specs=[pl.BlockSpec((cols, CC), lambda g: (0, g))] * 2,
        compiler_params=pltpu.CompilerParams(vmem_limit_bytes=58 * MIB),
        name="expand_columns",
    )(token, slots)


def assemble_kernel(step, token_ref, rows_ref, high_ref, low_ref, front_ref, out_ref):
    first = pl.program_id(0) * step
    place = lax.broadcasted_iota(jnp.int32, (step, rows_ref.shape[1]), 0) + first
    onehot = jnp.where(place == rows_ref[...], 1.0, 0.0).astype(BF16)
    out_ref[...] = front_ref[...] + (mm(onehot, high_ref[...], NT) + mm(onehot, low_ref[...], NT))


def assemble(front, rows, high, low, token):
    step = 256
    count, width = front.shape
    k = rows.shape[1]
    return pl.pallas_call(
        functools.partial(assemble_kernel, step),
        grid=(count // step,),
        out_shape=jax.ShapeDtypeStruct((count, width), F32),
        in_specs=[
            pl.BlockSpec(memory_space=pl.ANY),
            pl.BlockSpec((1, k), lambda i: (0, 0)),
            pl.BlockSpec((width, k), lambda i: (0, 0)),
            pl.BlockSpec((width, k), lambda i: (0, 0)),
            pl.BlockSpec((step, width), lambda i: (i, 0)),
        ],
        out_specs=pl.BlockSpec((step, width), lambda i: (i, 0)),
        compiler_params=pltpu.CompilerParams(vmem_limit_bytes=58 * MIB),
        name="assemble",
    )(token, rows, high, low, front)


def pick(cases, case_ref, at, target, sem):
    for number, source in cases:

        @pl.when(case_ref[at] == number)
        def _(source=source):
            copy(source, target, sem).start()


def pick(cases, who_ref, target, sem):
    for at, number, source in cases:

        @pl.when(who_ref[at] == number)
        def _(source=source):
            copy(source, target, sem).start()


def settle(cases, who_ref, target, sem):
    held = functools.reduce(jnp.logical_or, [who_ref[at] == number for at, number, _ in cases])

    @pl.when(held)
    def _():
        copy(target, target, sem).wait()


def view(ref, first, shape):
    return ref.at[pl.ds(first, shape[0]), pl.ds(0, shape[1])]


def solve_kernel(count, base, outer, plan, strip_plan, who_ref, token_ref, rows_ref, high_in, low_in, *refs):
    sources = refs[:count]
    out_high_ref, out_low_ref, raw_ref, inv_ref, high_ref, low_ref, piece_sem, strip_sem = refs[count:]

    def of(cases, shape):
        return [(at, n, view(sources[ref], f, shape)) for at, n, ref, f in cases]

    for k, (first, shape, cases) in enumerate(strip_plan):
        pick(of(cases, shape), who_ref, view(inv_ref, first, shape), strip_sem.at[k])
    for k, (first, shape, cases) in enumerate(plan):
        pick(of(cases, shape), who_ref, view(raw_ref, first - base, shape), piece_sem.at[k])
    for k, (first, shape, cases) in enumerate(strip_plan):
        target = view(inv_ref, first, shape)
        copy(target, target, strip_sem.at[k]).wait()
        part = (slice(first, first + shape[0]), slice(0, shape[1]))
        high_ref[part], low_ref[part] = halves(inv_ref[part])
    for k, (first, shape, cases) in enumerate(plan):
        settle(of(cases, shape), who_ref, view(raw_ref, first - base, shape), piece_sem.at[k])

    def part(i, _):
        rows = pl.ds(pl.multiple_of(i * STRIP, STRIP), STRIP)
        place = lax.broadcasted_iota(jnp.int32, (STRIP, rows_ref.shape[1]), 0) + i * STRIP + base
        onehot = jnp.where(place == rows_ref[...], 1.0, 0.0).astype(BF16)
        raw = raw_ref[rows, :] + (mm(onehot, high_in[...], NT) + mm(onehot, low_in[...], NT))
        a, b = halves(raw)
        for c in range(0, P_SIZE, STRIP):
            upto = c + STRIP
            high, low = high_ref[c:upto, :upto], low_ref[c:upto, :upto]
            total = mm(a[:, :upto], high, NT) + (mm(a[:, :upto], low, NT) + mm(b[:, :upto], high, NT))
            out_high_ref[rows, c:upto], out_low_ref[rows, c:upto] = halves(total)
        return 0

    start = jnp.where(who_ref[outer] == 0, max(0, P_SIZE - base) // STRIP, 0)
    lax.fori_loop(jnp.minimum(start, raw_ref.shape[0] // STRIP), raw_ref.shape[0] // STRIP, part, 0)


def solve(who, token, outer, rows, expanded, span, plan, strip_plan, arrays):
    base, count = span[0], span[1] - span[0]
    used = sorted({case[2] for _, _, cases in plan + strip_plan for case in cases})
    place = {ref: at for at, ref in enumerate(used)}

    def renumber(entries):
        return [
            (first, shape, [(at, n, place[ref], f) for at, n, ref, f in cases])
            for first, shape, cases in entries
        ]

    anywhere = pl.BlockSpec(memory_space=pl.ANY)
    resident = pl.BlockSpec(memory_space=VMEM)
    return pl.pallas_call(
        functools.partial(solve_kernel, len(used), base, outer, renumber(plan), renumber(strip_plan)),
        out_shape=[jax.ShapeDtypeStruct((count, P_SIZE), BF16)] * 2,
        in_specs=[pl.BlockSpec(memory_space=pltpu.SMEM), anywhere]
        + [resident] * 3
        + [anywhere] * len(used),
        out_specs=[resident] * 2,
        scratch_shapes=[
            VMEM((count, P_SIZE), F32),
            VMEM((P_SIZE, P_SIZE), F32),
            VMEM((P_SIZE, P_SIZE), BF16),
            VMEM((P_SIZE, P_SIZE), BF16),
            pltpu.SemaphoreType.DMA((len(plan),)),
            pltpu.SemaphoreType.DMA((len(strip_plan),)),
        ],
        compiler_params=pltpu.CompilerParams(vmem_limit_bytes=58 * MIB),
        cost_estimate=pl.CostEstimate(flops=2 * 10**10, bytes_accessed=2 * 10**7, transcendentals=0),
        name="solve_rows",
    )(who, token, rows, *expanded, *[arrays[ref] for ref in used])


def update_kernel(step, first_row, first_col, who_ref, rh_ref, rl_ref, ch_ref, cl_ref, front_ref, factor_ref, out_ref):
    above = (who_ref[0] == 0) & (pl.program_id(0) * step + first_row < P_SIZE)
    width = out_ref.shape[1]

    def schur(left):
        a, b = rh_ref[...], rl_ref[...]
        for c in range(left, width, WIDE):
            high, low = ch_ref[c : c + WIDE, :], cl_ref[c : c + WIDE, :]
            part = mm(a, high, NT) + (mm(a, low, NT) + mm(b, high, NT))
            out_ref[:, c : c + WIDE] = front_ref[:, c : c + WIDE] - part

    panel = (who_ref[1] == 0) if first_col == 0 else False

    @pl.when(above)
    def _():
        out_ref[...] = front_ref[...]

    if first_col == 0:

        @pl.when(above & panel)
        def _():
            out_ref[:, :P_SIZE] = factor_ref[...]

        @pl.when(jnp.logical_not(above) & panel)
        def _():
            out_ref[:, :P_SIZE] = rh_ref[...].astype(F32) + rl_ref[...].astype(F32)
            schur(P_SIZE)

    @pl.when(jnp.logical_not(above) & jnp.logical_not(panel))
    def _():
        schur(0)


def update(who, row_parts, col_parts, first_row, first_col, front, factor_rows):
    step = STRIP
    tall, wide = row_parts[0].shape[0], col_parts[0].shape[0]
    row = pl.BlockSpec((step, P_SIZE), lambda i: (i, 0))
    whole = pl.BlockSpec((wide, P_SIZE), lambda i: (0, 0))
    block = pl.BlockSpec((step, wide), lambda i: (i + first_row // step, first_col // wide))
    last = P_SIZE // step - 1
    return pl.pallas_call(
        functools.partial(update_kernel, step, first_row, first_col),
        grid=(tall // step,),
        out_shape=jax.ShapeDtypeStruct(front.shape, F32),
        in_specs=[
            pl.BlockSpec(memory_space=pltpu.SMEM),
            row,
            row,
            whole,
            whole,
            block,
            pl.BlockSpec((step, P_SIZE), lambda i: (jnp.minimum(i + first_row // step, last), 0)),
        ],
        out_specs=block,
        input_output_aliases={5: 0},
        compiler_params=pltpu.CompilerParams(vmem_limit_bytes=58 * MIB),
        name="schur_update",
    )(who, *row_parts, *col_parts, front, factor_rows)


BUFFER = 272
CARRIER = 2
FIRST = 1536
STRIPS = (512, 256, 256)
TOP_STEP = 1
TOP_END = 5
FACTOR_STEP = 2
INVERSE_ENDS = (5, 6, 7)
ASSEMBLE_STEP = 3
EXPAND_STEP = 9
SOLVE_STEP = 10
GATE_VMEM = 58


def move(part, pairs):
    return lax.ppermute(part, GRID, [(a * 4 + b, c * 4 + d) for (a, b), (c, d) in pairs])


def gate_kernel(fresh, held, who_ref, *refs):
    outs = refs[held : held + 1 + len(fresh)]
    stages, sems = refs[held + 1 + len(fresh) : -1], refs[-1]
    outs[0][...] = jnp.zeros_like(outs[0])

    def each(action):
        at = 0
        for k, (_, segments) in enumerate(fresh):
            for first, shape, cases in segments:
                action(k, at, first, shape, cases)
                at += 1

    def load(k, at, first, shape, cases):
        sources = [(where, n, view(refs[ref], f, shape)) for where, n, ref, f in cases]
        pick(sources, who_ref, view(stages[k], first, shape), sems.at[at])

    def loaded(k, at, first, shape, cases):
        settle([case[:3] for case in cases], who_ref, view(stages[k], first, shape), sems.at[at])

    def store(k, at, first, shape, cases):
        for where, n, _, _ in cases:

            @pl.when(who_ref[where] == n)
            def _():
                copy(view(stages[k], first, shape), view(outs[1 + k], first, shape), sems.at[at]).start()

    each(load)
    each(loaded)
    each(store)
    each(loaded)


class Line:
    def __init__(self, who):
        self.who = who
        self.token = jnp.zeros((8, 128), F32)

    def gate(self, arrived, fresh=()):
        arrays = [self.token] + list(arrived)

        def place(array):
            for k, other in enumerate(arrays):
                if other is array:
                    return k
            arrays.append(array)
            return len(arrays) - 1

        entries = [
            (shape, [(f, size, [(at, n, place(a), r) for at, n, a, r in cases]) for f, size, cases in segments])
            for shape, segments in fresh
        ]
        anywhere = pl.BlockSpec(memory_space=pl.ANY)
        parts = max(1, sum(len(segments) for _, segments in entries))
        out = pl.pallas_call(
            functools.partial(gate_kernel, entries, len(arrays)),
            out_shape=[jax.ShapeDtypeStruct((8, 128), F32)]
            + [jax.ShapeDtypeStruct(shape, F32) for shape, _ in entries],
            in_specs=[pl.BlockSpec(memory_space=pltpu.SMEM)] + [anywhere] * len(arrays),
            out_specs=[pl.BlockSpec(memory_space=VMEM)] + [anywhere] * len(entries),
            scratch_shapes=[VMEM(shape, F32) for shape, _ in entries] + [pltpu.SemaphoreType.DMA((parts,))],
            compiler_params=pltpu.CompilerParams(vmem_limit_bytes=GATE_VMEM * MIB),
            name="gate",
        )(self.who, *arrays)
        self.token = out[0]
        return out[1:]


def pieces_of(rows, tile_rows):
    sizes, left = [], rows
    while left > 0:
        room = BUFFER - tile_rows if len(sizes) == CARRIER else BUFFER
        sizes.append(min(room, left))
        left -= sizes[-1]
    return sizes


def fast_local(front_block, child_tiles, child_rows, child_cols, child_owner):
    front = front_block[0]
    block_rows, block_cols = front.shape
    row = lax.axis_index("row")
    col = lax.axis_index("col")
    away = row ^ col
    low = (1, 2, 3)
    bottom = block_rows - P_SIZE
    yes = lambda flag: jnp.where(flag, 1, 0)
    mine = row * 4 + col
    along = jnp.where(col == 0, yes(row > 0), jnp.where((row == 0) & (col == 1), 3, jnp.where(col < 3, 2, 0)))
    round_zero = jnp.where(row == 1, 3, jnp.where(row == 3, 2, 0))
    round_low = jnp.where(away == 0, 1, jnp.where(away == 1, 2, 0))
    who = jnp.stack(
        [
            row,
            col,
            mine,
            yes(mine == 0),
            along,
            jnp.where(col == 0, round_zero, round_low),
            jnp.where(row == 0, col, 4),
            jnp.where(col == 0, 0, mine),
        ]
    ).astype(jnp.int32)
    line = Line(who)
    arrays = [front]

    def use(array):
        for ref, other in enumerate(arrays):
            if other is array:
                return ref
        arrays.append(array)
        return len(arrays) - 1

    known = {}
    ends = {}
    steps = {}

    def until(step, *moved):
        ends.setdefault(step, []).extend(moved)

    def do(step, action):
        steps.setdefault(step, []).append(action)

    slots = pack(child_tiles[0], child_rows[0], child_cols[0], child_owner[0], 16)
    slots = lax.all_to_all(slots, GRID, split_axis=0, concat_axis=0, tiled=True)
    flat = slots.reshape(-1, P_SIZE)
    tile_rows = flat.shape[0]

    def rows_of(array):
        return array[:, CR + 1, :CR].astype(jnp.int32).reshape(1, -1)

    plans = {"row": [], "col": []}
    tiles = {"row": [(7, 0, flat, 0)], "col": [(2, 0, flat, 0)]}

    def found(name, first, rows, where, number, array, inner):
        plans[name].append((first, rows, where, number, array, inner))

    sizes = pieces_of(block_rows, tile_rows)
    count = len(sizes)
    tops = [sum(sizes[:k]) for k in range(count)]
    found("row", 0, block_rows, 7, 0, front, 0)
    found("col", bottom, P_SIZE, 2, 0, front, bottom)
    zero_rows = P_SIZE + tile_rows
    zero_count = -(-zero_rows // BUFFER)
    hops = {"z": {}, "xd": {}, "y": {}}

    def arrived_low(k):
        def hold(name, number, array):
            found(name, tops[k], sizes[k], 2, number, array, 0)
            if k == CARRIER:
                tiles[name].append((2, number, array, sizes[k]))

        for r in low:
            for c in low:
                hold("row", r * 4 + c, hops["z"][k + c - 1])
        for c in low:
            hold("col", c * 4 + c, hops["z"][k + c - 1])
            hold("col", (c ^ 1) * 4 + c, hops["xd"][k + c])
            hold("col", (c ^ 2) * 4 + c, hops["y"][k + c])
            hold("col", (c ^ 3) * 4 + c, hops["xd"][k + c + 1])

    zero_hops = {"row": (1, ((2, "z", 0), (3, "z", 1))), "col": (4, ((12, "xd", 0), (8, "xd", 1)))}

    def arrived_zero_tiles():
        for name, (near, others) in zero_hops.items():
            tiles[name].append((2, near, known["zero", name], 0))
            for number, kind, late in others:
                tiles[name].append((2, number, hops[kind][TOP_END + late], 0))

    def arrived_zero(j):
        for name, (near, others) in zero_hops.items():
            first, last = max(0, j * BUFFER - tile_rows), min((j + 1) * BUFFER, zero_rows) - tile_rows
            inner = first + tile_rows - j * BUFFER
            found(name, bottom + first, last - first, 2, near, known["zero", name], first + tile_rows)
            for number, kind, late in others:
                found(name, bottom + first, last - first, 2, number, hops[kind][TOP_END + j + late], inner)

    def z_fresh(step):
        segments = []
        whole = (BUFFER, P_SIZE)
        if step > 0:
            segments.append((0, whole, [(4, 2, hops["z"][step - 1], 0)]))
        if step < count:
            segments.append((0, (sizes[step], P_SIZE), [(4, 1, front, tops[step])]))
            if step == CARRIER:
                segments.append((sizes[step], (tile_rows, P_SIZE), [(4, 1, flat, 0)]))
        segments += zero_segments(step, "row", 4)
        return (whole, segments)

    def zero_segments(step, name, place):
        j = step - TOP_END
        if 0 <= j < zero_count:
            tall = min(BUFFER, zero_rows - j * BUFFER)
            return [(0, (tall, P_SIZE), [(place, 3, known["zero", name], j * BUFFER)])]
        return []

    def xd_fresh(step):
        whole = (BUFFER, P_SIZE)
        segments = [(0, whole, [(5, 1, hops["z"][step - 1], 0)])]
        if step - 1 in hops["xd"]:
            segments.append((0, whole, [(5, 2, hops["xd"][step - 1], 0)]))
        return (whole, segments + zero_segments(step, "col", 5))

    def z_move(step, part):
        pairs = []
        for c in range(3):
            if 0 <= step - c < count:
                pairs += [((r, c), (r, c + 1)) for r in low]
            if c > 0 and 0 <= step - (c - 1) - TOP_END < zero_count:
                pairs.append(((0, c), (0, c + 1)))
        hops["z"][step] = move(part, pairs)
        until(step + 1, hops["z"][step])

    def xd_move(step, part):
        pairs = []
        for c in low:
            if 0 <= step - c < count:
                pairs.append(((c, c), (c ^ 1, c)))
            if 0 <= step - c - 1 < count:
                pairs.append(((c ^ 1, c), (c ^ 3, c)))
        if 0 <= step - TOP_END < zero_count:
            pairs.append(((1, 0), (3, 0)))
        if 0 <= step - 1 - TOP_END < zero_count:
            pairs.append(((3, 0), (2, 0)))
        hops["xd"][step] = move(part, pairs)
        until(step + 1, hops["xd"][step])

    def y_move(step):
        pairs = [((c, c), (c ^ 2, c)) for c in low if 0 <= step - c < count]
        if pairs:
            hops["y"][step] = move(hops["z"][step - 1], pairs)
            until(step + 1, hops["y"][step])

    def top(part):
        known["zero", "row"] = move(part, [((0, 0), (0, 1))])
        known["zero", "col"] = move(part, [((0, 0), (1, 0))])
        until(TOP_END, known["zero", "row"], known["zero", "col"])

    holds = yes(mine == 0).reshape(1)
    strip_plan = []
    wanted = {}

    def factoring():
        known["rows"] = rows_of(slots)
        panel = expand(slots, P_SIZE, line.token)
        state = [front, known["rows"], *panel]
        for at, tall in enumerate(STRIPS):
            first = sum(STRIPS[:at])
            z_state, known["factor"], strip = factor(first, tall, holds, line.token, state, P_SIZE)
            state = [z_state, known["factor"]]
            two = move(strip, [((0, 0), (0, 2))])
            step = INVERSE_ENDS[at]
            until(step, two)
            want(step, strip.shape, [(2, 0, strip, 0), (2, 2, two, 0)], functools.partial(inverse_across, step, first))

    def want(step, shape, cases, action):
        wanted.setdefault(step, []).append(((shape, [(0, shape, cases)]), action))

    def inverse_across(step, first, part):
        other = move(part, [((0, 0), (0, 1)), ((0, 2), (0, 3))])
        until(step + 1, other)
        cases = [(6, c, (part, other)[c % 2], 0) for c in range(4)]
        want(step + 1, part.shape, cases, functools.partial(inverse_plane, step + 1, first))

    def inverse_plane(step, first, part):
        near = move(part, [((0, c), (1, c)) for c in range(4)])
        until(step + 1, near)
        cases = [(0, 0, part, 0), (0, 1, near, 0)]
        want(step + 1, part.shape, cases, functools.partial(inverse_far, step + 1, first))

    def inverse_far(step, first, part):
        far = move(part, [((r, c), (r + 2, c)) for r in (0, 1) for c in range(4)])
        until(step + 1, far)
        strip_plan.append((first, part.shape, [(0, r, use((part, far)[r // 2]), 0) for r in range(4)]))

    def assembling():
        parts = expand(slots, block_cols, line.token)
        known["assembled"] = assemble(front, known["rows"], *parts, line.token)

    def expanding(row_part, col_part):
        for name, part in (("row", row_part), ("col", col_part)):
            own = part.reshape(slots.shape)
            known[name] = (rows_of(own), expand(own, P_SIZE, line.token))

    groups = (0, FIRST, block_rows)
    solved = {}

    def solving(group, name):
        low_end, high_end = groups[group], groups[group + 1]
        plan = {}
        for first, rows, where, number, array, inner in plans[name]:
            a, b = max(first, low_end), min(first + rows, high_end)
            if a < b:
                plan.setdefault((a, b), []).append((where, number, use(array), inner + a - first))
        entries = [(a, (b - a, P_SIZE), cases) for (a, b), cases in plan.items()]
        outer = 0 if name == "row" else 1
        solved[name, group] = solve(
            who, line.token, outer, *known[name], (low_end, high_end), entries, strip_plan, arrays
        )

    def updating(a, b):
        known["assembled"] = update(
            who, solved["row", a], solved["col", b], groups[a], groups[b], known["assembled"], known["factor"]
        )

    last = max(count + 4, TOP_END + zero_count + 1)
    for step in range(last + 1):
        fresh, uses = [], []

        def wants(entry, action):
            fresh.append(entry)
            uses.append(action)

        if step < max(count + 2, TOP_END + zero_count + 1):
            wants(z_fresh(step), functools.partial(z_move, step))
        if 0 < step < last:
            wants(xd_fresh(step), functools.partial(xd_move, step))
        if step == TOP_STEP:
            segments = [(0, (tile_rows, P_SIZE), [(3, 1, flat, 0)])]
            segments.append((tile_rows, (P_SIZE, P_SIZE), [(3, 1, front, bottom)]))
            wants(((zero_rows, P_SIZE), segments), top)
        for entry, action in wanted.get(step, []):
            wants(entry, action)
        if step == EXPAND_STEP:
            arrived_low(CARRIER)
            arrived_zero_tiles()
            for name in ("row", "col"):
                shape = (tile_rows, P_SIZE)
                wants((shape, [(0, shape, tiles[name])]), lambda part, name=name: known.__setitem__(("tiles", name), part))
        out = line.gate(ends.get(step, []), fresh)
        for part, action in zip(out, uses):
            action(part)
        if 0 < step < last:
            y_move(step)
        for action in steps.get(step, []):
            action()
        if step == FACTOR_STEP:
            factoring()
        if step == ASSEMBLE_STEP:
            assembling()
            until(step + 1, known["assembled"])
        if step == EXPAND_STEP:
            expanding(known["tiles", "row"], known["tiles", "col"])
        if step == SOLVE_STEP:
            for k in range(count):
                if k != CARRIER and tops[k] < FIRST:
                    arrived_low(k)
            early = [j for j in range(zero_count) if bottom + j * BUFFER - tile_rows < FIRST]
            for j in early:
                arrived_zero(j)
            solving(0, "row")
            solving(0, "col")
    for k in range(count):
        if tops[k] >= FIRST:
            arrived_low(k)
    for j in range(len(early), zero_count):
        arrived_zero(j)
    updating(0, 0)
    solving(1, "row")
    solving(1, "col")
    updating(0, 1)
    updating(1, 0)
    updating(1, 1)
    return known["assembled"][None]


def blocked_factor(symmetric):
    count = symmetric.shape[0] // DB
    remaining = symmetric
    columns = []
    inverses = []
    identity = jnp.eye(DB, dtype=symmetric.dtype)
    for step in range(count):
        start = step * DB
        chol = jnp.linalg.cholesky(remaining[:DB, :DB])
        inverse = lax.linalg.triangular_solve(chol, identity, left_side=True, lower=True)
        below = jnp.dot(remaining[DB:, :DB], inverse.T, precision=lax.Precision.HIGHEST)
        remaining = remaining[DB:, DB:] - jnp.dot(below, below.T, precision=lax.Precision.HIGHEST)
        columns.append(jnp.concatenate([jnp.zeros((start, DB), symmetric.dtype), chol, below], 0))
        inverses.append(inverse)
    return (jnp.concatenate(columns, 1), inverses)


def blocked_solve(panel, factor, inverses):
    solved_parts = []
    for step in range(len(inverses)):
        start = step * DB
        rhs = panel[:, start : start + DB]
        if step > 0:
            earlier = jnp.concatenate(solved_parts, 1)
            rhs = rhs - jnp.dot(
                earlier, factor[start : start + DB, :start].T, precision=lax.Precision.HIGHEST
            )
        solved_parts.append(jnp.dot(rhs, inverses[step].T, precision=lax.Precision.HIGHEST))
    return jnp.concatenate(solved_parts, 1)


def local(front_block, child_tiles, child_rows, child_cols, child_owner):
    front_part = front_block[0]
    child_part = child_tiles[0]
    row_maps = child_rows[0]
    col_maps = child_cols[0]
    owners = child_owner[0]
    row_count = lax.axis_size("row")
    col_count = lax.axis_size("col")
    group_count = row_count * col_count
    block_rows, block_cols = front_part.shape
    tile_count = owners.shape[0]
    positions = jnp.arange(tile_count)
    earlier = (owners[:, None] == owners[None, :]) & (positions[None, :] < positions[:, None])
    tile_rank = jnp.sum(earlier.astype(jnp.int32), axis=1)
    slot_index = owners * CAP + tile_rank
    send_tiles = (
        jnp.zeros((group_count * CAP, CR, CC), front_part.dtype).at[slot_index].set(child_part)
    )
    send_rows = jnp.zeros((group_count * CAP, CR), jnp.int32).at[slot_index].set(row_maps)
    send_cols = jnp.zeros((group_count * CAP, CC), jnp.int32).at[slot_index].set(col_maps)
    recv_tiles, recv_rows, recv_cols = (
        lax.all_to_all(send_tiles, ("row", "col"), split_axis=0, concat_axis=0, tiled=True),
        lax.all_to_all(send_rows, ("row", "col"), split_axis=0, concat_axis=0, tiled=True),
        lax.all_to_all(send_cols, ("row", "col"), split_axis=0, concat_axis=0, tiled=True),
    )
    assembled = front_part.at[recv_rows[:, :, None], recv_cols[:, None, :]].add(recv_tiles)
    panel_block = spread(assembled[:, :P_SIZE], "col", 0)
    row_index = lax.axis_index("row")
    col_index = lax.axis_index("col")
    first_row = row_index * block_rows
    held_rows = min(P_SIZE, block_rows)
    holders = max(1, P_SIZE // block_rows)
    diag_pieces = [spread(panel_block[:held_rows], "row", member) for member in range(holders)]
    diag_block = jnp.concatenate(diag_pieces, 0)
    symmetric = 0.5 * (diag_block + diag_block.T)
    factor, inverses = blocked_factor(symmetric)
    solved = blocked_solve(panel_block, factor, inverses)
    global_rows = first_row + jnp.arange(block_rows)
    below_mask = global_rows[:, None] >= P_SIZE
    if block_rows <= P_SIZE:
        factor_rows = lax.dynamic_slice_in_dim(
            factor, jnp.minimum(first_row, P_SIZE - block_rows), block_rows, 0
        )
    else:
        factor_rows = jnp.concatenate(
            [factor, jnp.zeros((block_rows - P_SIZE, P_SIZE), factor.dtype)], 0
        )
    panel_out = jnp.where(below_mask, solved, factor_rows)
    lower_part = jnp.where(below_mask, solved, 0.0)
    group_ratio = row_count // col_count
    column_parts = [
        spread(lower_part, "row", col_index * group_ratio + member) for member in range(group_ratio)
    ]
    column_part = jnp.concatenate(column_parts, 0)
    schur_block = assembled - jnp.dot(lower_part, column_part.T, precision=lax.Precision.HIGHEST)
    global_cols = col_index * block_cols + jnp.arange(block_cols)
    left_part = jnp.concatenate(
        [panel_out, jnp.zeros((block_rows, block_cols - P_SIZE), panel_out.dtype)], 1
    )
    trailing = below_mask & (global_cols[None, :] >= P_SIZE)
    updated = jnp.where(
        global_cols[None, :] < P_SIZE, left_part, jnp.where(trailing, schur_block, assembled)
    )
    return updated[None]


def solution(mesh):
    placed = (
        P("front", "row", "col"),
        P("front", ("row", "col"), None, None),
        P("front", ("row", "col"), None),
        P("front", ("row", "col"), None),
        P("front", ("row", "col")),
    )
    square = mesh.shape["row"] == 4 and mesh.shape["col"] == 4
    return jax.shard_map(
        fast_local if square else local,
        mesh=mesh,
        in_specs=placed,
        out_specs=P("front", "row", "col"),
        check_vma=False,
    )
```
